32 devices in a mesh: ctx: 4 (over z), fsdp: 8 (over y, x, core).
Axes of the slice: x: 2, y: 2, z: 4, core: 2. Of those that a mesh axis runs over, the one named last changes fastest.
Arguments:
- hidden_in: bfloat16 [24, 1024, 768], P('fsdp', 'ctx'), may hold values from -6 to 6
- attn_gain: bfloat16 [768], P('fsdp'), may hold values from 0.099609375 to 1.8984375
- attn_shift: bfloat16 [768], P('fsdp'), may hold values from -1.75 to 1.75
- query_key_value_weight: bfloat16 [768, 2304], P('fsdp'), may hold values from -0.21875 to 0.21875
- query_bias: bfloat16 [768], P('fsdp'), may hold values from -1.75 to 1.75
- value_bias: bfloat16 [768], P('fsdp'), may hold values from -1.75 to 1.75
- projection_output_weight: bfloat16 [768, 768], P('fsdp'), may hold values from -1.75 to 1.75
- projection_output_bias: bfloat16 [768], P('fsdp'), may hold values from -1.75 to 1.75
- mlp_gain: bfloat16 [768], P('fsdp'), may hold values from 0.099609375 to 1.8984375
- mlp_shift: bfloat16 [768], P('fsdp'), may hold values from -1.75 to 1.75
- up_projection_weight: bfloat16 [768, 3072], P('fsdp'), may hold values from -0.21875 to 0.21875
- up_projection_bias: bfloat16 [3072], P('fsdp'), may hold values from -1.75 to 1.75
- down_projection_weight: bfloat16 [3072, 768], P('fsdp'), may hold values from -0.109375 to 0.109375
- down_projection_bias: bfloat16 [768], P('fsdp'), may hold values from -1.75 to 1.75
- out_grad: bfloat16 [24, 1024, 768], P('fsdp', 'ctx'), may hold values from -8 to 8
Outputs:
- block_out: bfloat16 [24, 1024, 768], P('fsdp', 'ctx')
- input_grad: bfloat16 [24, 1024, 768], P('fsdp', 'ctx')
- attn_gain_grad: float32 [768], P('fsdp')
- attn_shift_grad: float32 [768], P('fsdp')
- qkv_grad: float32 [768, 2304], P('fsdp')
- query_bias_grad: float32 [768], P('fsdp')
- value_bias_grad: float32 [768], P('fsdp')
- proj_grad: float32 [768, 768], P('fsdp')
- proj_bias_grad: float32 [768], P('fsdp')
- mlp_gain_grad: float32 [768], P('fsdp')
- mlp_shift_grad: float32 [768], P('fsdp')
- up_grad: float32 [768, 3072], P('fsdp')
- up_bias_grad: float32 [3072], P('fsdp')
- down_grad: float32 [3072, 768], P('fsdp')
- down_bias_grad: float32 [768], P('fsdp')
- softmax_stats: float32 [24, 12, 1024], P('fsdp', None, 'ctx')
The draws below stay inside these ranges and needn't reach their ends.
All inputs are finite; a program needn't handle non-finite values.
Results may differ from the reference program's by a relative error of at most 0.033.
Values may be sent and summed in bfloat16 or wider, within the bound.
A program may use at most 192 MiB of HBM per device.

```python
import jax
import jax.numpy as jnp
from jax import lax

D = 768
HEADS = 12
HD = 64
FF = 3072
SEQS = 24
LEN = 1024


def strengthened(array, key, source, target, shards_of, factor):
    owner, partner = [(jnp.arange(array.shape[axis_at]) // (array.shape[axis_at] // shards_of)).reshape([-1 if axis == axis_at else 1 for axis in range(array.ndim)]) for axis_at in (source, target)]
    chosen = jax.random.permutation(key, shards_of)[partner]
    strong = (owner == chosen) | (owner == (partner + shards_of // 2) % shards_of)
    return jnp.where(strong, factor * array, array)


def shard_levels(rng, extent, cuts, smallest, largest):
    def one(dim, blocks):
        steps = jax.random.uniform(jax.random.fold_in(jax.random.fold_in(rng, 6), dim), (blocks,), jnp.float32, smallest / len(cuts), largest / len(cuts))
        return jnp.repeat(jnp.exp(steps), extent[dim] // blocks).reshape((-1,) + (1,) * (len(extent) - dim - 1))

    level = one(*cuts[0])
    for cut in cuts[1:]:
        level = level * one(*cut)
    return level


def normal_values(key, shape, deviation, most, shards=(), held_as=jnp.bfloat16):
    loudness = shard_levels(key, shape, shards, -0.22, 0.18) if shards else 1.0
    drawn = jax.random.normal(key, shape, jnp.float32) * deviation * loudness
    return jnp.minimum(jnp.maximum(drawn, -most), most).astype(held_as)


def bell_draw_with(key, dims, deviation, most, cuts, heavy, dtype=jnp.bfloat16):
    array = deviation * jax.random.normal(key, dims, jnp.float32)
    if cuts:
        array = array * shard_levels(key, dims, cuts, -0.22, 0.18)
    return jnp.clip(strengthened(array, jax.random.fold_in(key, 3), *heavy), -most, most).astype(dtype)


def setup_inputs(seed: int = 0) -> dict:
    key_of = jax.random.split(jax.random.key(seed), 16)
    return {
        "hidden_in": normal_values(key_of[0], (SEQS, LEN, D), 1.0, 6.0, ((0, 8), (1, 4))),
        "attn_gain": jnp.clip(1.0 + 0.18 * jax.random.normal(key_of[1], (D,), jnp.float32), 0.099609375, 1.8984375).astype(jnp.bfloat16),
        "attn_shift": normal_values(key_of[2], (D,), 0.3, 1.75, ((0, 8),)),
        "query_key_value_weight": normal_values(key_of[3], (D, 3 * D), D ** -0.5, 0.21875, ((0, 8),)),
        "query_bias": normal_values(key_of[4], (D,), 0.3, 1.75, ((0, 8),)),
        "value_bias": normal_values(key_of[5], (D,), 0.3, 1.75, ((0, 8),)),
        "projection_output_weight": normal_values(key_of[6], (D, D), (D // 64) ** -0.5, 1.75, ((0, 8),)),
        "projection_output_bias": normal_values(key_of[7], (D,), 0.3, 1.75, ((0, 8),)),
        "mlp_gain": jnp.clip(1.0 + 0.18 * jax.random.normal(key_of[8], (D,), jnp.float32), 0.099609375, 1.8984375).astype(jnp.bfloat16),
        "mlp_shift": normal_values(key_of[9], (D,), 0.3, 1.75, ((0, 8),)),
        "up_projection_weight": normal_values(key_of[10], (D, FF), D ** -0.5, 0.21875, ((0, 8),)),
        "up_projection_bias": normal_values(key_of[11], (FF,), 0.3, 1.75, ((0, 8),)),
        "down_projection_weight": normal_values(key_of[12], (FF, D), FF ** -0.5, 0.109375, ((0, 8),)),
        "down_projection_bias": normal_values(key_of[13], (D,), 0.3, 1.75, ((0, 8),)),
        "out_grad": bell_draw_with(key_of[14], (SEQS, LEN, D), 1.0, 8.0, ((0, 8), (1, 4)), (0, 2, 8, 2.0)),
    }


@jax.custom_vjp
def low(v):
    return lax.optimization_barrier(v.astype(jnp.bfloat16)).astype(jnp.float32)

@jax.custom_vjp
def lowered_backward(v):
    return v

def low_keep(v):
    return (low(v), None)

def low_pass(kept, grad):
    return (grad,)

def back_keep(v):
    return (v, None)

def back_low(kept, grad):
    return (low(grad),)
low.defvjp(low_keep, low_pass)
lowered_backward.defvjp(back_keep, back_low)
HIGH_PRECISION = lax.Precision.HIGHEST
NEG_BIG = -1e+30

def layer_norm(values, gain, shift):
    center = values - lax.optimization_barrier(jnp.mean(values, axis=-1, keepdims=True))
    spread = lax.optimization_barrier(jnp.mean(center * center, axis=-1, keepdims=True))
    return center * lax.rsqrt(spread + 1e-05) * gain + shift

def attend_sequence(inputs):
    queries, key_rows, values = inputs
    seq_length = queries.shape[0]
    query_heads = queries.reshape(seq_length, HEADS, HD)
    key_heads = key_rows.reshape(seq_length, HEADS, HD)
    value_heads = values.reshape(seq_length, HEADS, HD)
    scores = lowered_backward(jnp.einsum('qhe,khe->hqk', query_heads, key_heads, precision=HIGH_PRECISION))
    places = jnp.arange(seq_length)
    visible = places[:, None] >= places[None, :]
    scores = jnp.where(visible[None], scores, NEG_BIG)
    row_max = lax.optimization_barrier(jnp.max(scores, axis=-1, keepdims=True))
    weights = jnp.exp(scores - row_max)
    row_sum = lax.optimization_barrier(jnp.sum(weights, axis=-1, keepdims=True))
    mixed_heads = jnp.einsum('hqk,khe->hqe', low(weights), value_heads, precision=HIGH_PRECISION) / row_sum
    attended_rows = jnp.transpose(mixed_heads, (1, 0, 2)).reshape(seq_length, HEADS * HD)
    return (attended_rows, (row_max + jnp.log(row_sum))[..., 0])

def forward(hidden, params):
    attn_gain, attn_shift, query_key_value_weight, query_bias, value_bias, projection_output_weight, projection_output_bias, mlp_gain, mlp_shift, up_projection_weight, up_projection_bias, down_projection_weight, down_projection_bias = params
    normed_input = low(layer_norm(hidden, attn_gain, attn_shift))
    joined_heads = jnp.einsum('gea,az->gez', normed_input, query_key_value_weight, precision=HIGH_PRECISION)
    queries = low(lowered_backward((joined_heads[..., :D] + query_bias) * 0.125))
    key_rows = low(lowered_backward(joined_heads[..., D:2 * D]))
    values = low(lowered_backward(joined_heads[..., 2 * D:] + value_bias))
    attended_rows, row_stats = lax.map(jax.checkpoint(attend_sequence), (queries, key_rows, values))
    attended_rows = low(lowered_backward(attended_rows))
    branch_output = lowered_backward(jnp.einsum('gpb,bi->gpi', attended_rows, projection_output_weight, precision=HIGH_PRECISION) + projection_output_bias)
    middle_residual = hidden + branch_output
    second_normed = low(layer_norm(middle_residual, mlp_gain, mlp_shift))
    inner_preactivation = lowered_backward(jnp.einsum('gea,az->gez', second_normed, up_projection_weight, precision=HIGH_PRECISION) + up_projection_bias)
    active_hidden = low(jax.nn.gelu(inner_preactivation, approximate=False))
    block_result = middle_residual + lowered_backward(jnp.einsum('emi,ir->emr', active_hidden, down_projection_weight, precision=HIGH_PRECISION) + down_projection_bias)
    return (block_result, row_stats)

def reference(hidden_in, attn_gain, attn_shift, query_key_value_weight, query_bias, value_bias, projection_output_weight, projection_output_bias, mlp_gain, mlp_shift, up_projection_weight, up_projection_bias, down_projection_weight, down_projection_bias, out_grad):
    params = tuple((piece.astype(jnp.float32) for piece in (attn_gain, attn_shift, query_key_value_weight, query_bias, value_bias, projection_output_weight, projection_output_bias, mlp_gain, mlp_shift, up_projection_weight, up_projection_bias, down_projection_weight, down_projection_bias)))
    hidden = hidden_in.astype(jnp.float32)
    block_result, pullback, row_stats = jax.vjp(forward, hidden, params, has_aux=True)
    grad_hidden, grad_params = pullback(out_grad.astype(jnp.float32))
    return (block_result.astype(jnp.bfloat16), grad_hidden.astype(jnp.bfloat16), grad_params[0], grad_params[1], grad_params[2], grad_params[3], grad_params[4], grad_params[5], grad_params[6], grad_params[7], grad_params[8], grad_params[9], grad_params[10], grad_params[11], grad_params[12], row_stats)
```

```python
from functools import partial

import jax
import jax.numpy as jnp
from jax import lax
from jax.experimental import pallas as pl
from jax.experimental.pallas import tpu as pltpu
from jax.sharding import PartitionSpec as P

HEADS = 12
HD = 64


NEG_BIG = -1e30


def as_sent(value):
    return jax.tree.map(lambda a: a.astype(jnp.bfloat16) if a.dtype == jnp.float32 else a, value)


def layer_norm(values, gain, shift):
    center = values - jnp.mean(values, axis=-1, keepdims=True)
    spread = jnp.mean(center * center, axis=-1, keepdims=True)
    return center * lax.rsqrt(spread + 1e-05) * gain + shift


def exact_gelu(values):
    return jax.nn.gelu(values, approximate=False)


def split_heads(values):
    return values.reshape(values.shape[0], values.shape[1], HEADS, HD)


def forward_block(carry_state, blocks, key_start, queries, query_pos):
    keys_blk, values_blk = blocks

    def forward_update(unused):
        run_max, run_sum, accumulated = carry_state
        scores = jnp.einsum(
            "sbhe,snhe->shbn", queries, split_heads(keys_blk), preferred_element_type=jnp.float32
        )
        key_pos = key_start + jnp.arange(keys_blk.shape[1])
        visible = query_pos[:, None] >= key_pos[None, :]
        scores = jnp.where(visible, scores, NEG_BIG)
        new_max = jnp.maximum(run_max, jnp.max(scores, axis=-1))
        weights = jnp.where(visible, jnp.exp(scores - new_max[..., None]), 0.0)
        factor = jnp.exp(run_max - new_max)
        new_sum = run_sum * factor + jnp.sum(weights, axis=-1)
        new_acc = accumulated * factor[..., None] + jnp.einsum(
            "shbn,snhe->shbe",
            weights.astype(jnp.bfloat16),
            split_heads(values_blk),
            preferred_element_type=jnp.float32,
        )
        return (new_max, new_sum, new_acc)

    return lax.cond(key_start > query_pos[-1], lambda unused: carry_state, forward_update, None)


def query_block(carry_state, blocks, key_start, queries, grad_out, row_stats, row_delta, query_pos):
    keys_blk, values_blk = blocks

    def query_update(unused):
        query_grad = carry_state[0]
        key_heads = split_heads(keys_blk)
        scores = jnp.einsum(
            "sbhe,snhe->shbn", queries, key_heads, preferred_element_type=jnp.float32
        )
        key_pos = key_start + jnp.arange(keys_blk.shape[1])
        visible = query_pos[:, None] >= key_pos[None, :]
        probability = jnp.where(visible, jnp.exp(scores - row_stats[..., None]), 0.0)
        prob_grad = jnp.einsum(
            "sbhe,snhe->shbn", grad_out, split_heads(values_blk), preferred_element_type=jnp.float32
        )
        score_grad = (probability * (prob_grad - row_delta[..., None])).astype(jnp.bfloat16)
        return (
            query_grad
            + jnp.einsum(
                "shbn,snhe->shbe", score_grad, key_heads, preferred_element_type=jnp.float32
            ),
        )

    return lax.cond(key_start > query_pos[-1], lambda unused: carry_state, query_update, None)


def key_block(
    carry_state,
    query_blk,
    grad_blk,
    stats_blk,
    delta_blk,
    query_start,
    key_heads,
    value_heads,
    key_pos,
):
    query_pos = query_start + jnp.arange(query_blk.shape[1])

    def key_update(unused):
        key_grad, value_grad = carry_state
        stats_now = jnp.transpose(stats_blk, (0, 2, 1))
        delta_now = jnp.transpose(delta_blk, (0, 2, 1))
        scores = jnp.einsum(
            "sbhe,snhe->shbn", query_blk, key_heads, preferred_element_type=jnp.float32
        )
        visible = query_pos[:, None] >= key_pos[None, :]
        probability = jnp.where(visible, jnp.exp(scores - stats_now[..., None]), 0.0)
        value_grad = value_grad + jnp.einsum(
            "shbn,sbhe->snhe",
            probability.astype(jnp.bfloat16),
            grad_blk,
            preferred_element_type=jnp.float32,
        )
        prob_grad = jnp.einsum(
            "sbhe,snhe->shbn", grad_blk, value_heads, preferred_element_type=jnp.float32
        )
        score_grad = (probability * (prob_grad - delta_now[..., None])).astype(jnp.bfloat16)
        key_grad = key_grad + jnp.einsum(
            "shbn,sbhe->snhe", score_grad, query_blk, preferred_element_type=jnp.float32
        )
        return (key_grad, value_grad)

    return lax.cond(query_pos[-1] < key_pos[0], lambda unused: carry_state, key_update, None)


def sweep_blocks(carry_state, arrays, first_row, block_rows, step):
    block_count = arrays[0].shape[1] // block_rows

    def one_block(block_num, carry):
        offset = block_num * block_rows
        blocks = tuple((lax.dynamic_slice_in_dim(array, offset, block_rows, 1) for array in arrays))
        return step(carry, blocks, first_row + offset)

    return lax.fori_loop(0, block_count, one_block, carry_state)


def local_general(
    hidden_in,
    attn_gain,
    attn_shift,
    query_key_value_weight,
    query_bias,
    value_bias,
    projection_output_weight,
    projection_output_bias,
    mlp_gain,
    mlp_shift,
    up_projection_weight,
    up_projection_bias,
    down_projection_weight,
    down_projection_bias,
    out_grad,
):
    (
        attn_gain_all,
        attn_shift_all,
        qkv_weight_all,
        query_bias_all,
        value_bias_all,
        proj_weight_all,
        proj_bias_all,
        mlp_gain_all,
        mlp_shift_all,
        up_weight_all,
        up_bias_all,
        down_weight_all,
        down_bias_all,
    ) = (
        lax.all_gather(attn_gain, "fsdp", axis=0, tiled=True),
        lax.all_gather(attn_shift, "fsdp", axis=0, tiled=True),
        lax.all_gather(query_key_value_weight, "fsdp", axis=0, tiled=True),
        lax.all_gather(query_bias, "fsdp", axis=0, tiled=True),
        lax.all_gather(value_bias, "fsdp", axis=0, tiled=True),
        lax.all_gather(projection_output_weight, "fsdp", axis=0, tiled=True),
        lax.all_gather(projection_output_bias, "fsdp", axis=0, tiled=True),
        lax.all_gather(mlp_gain, "fsdp", axis=0, tiled=True),
        lax.all_gather(mlp_shift, "fsdp", axis=0, tiled=True),
        lax.all_gather(up_projection_weight, "fsdp", axis=0, tiled=True),
        lax.all_gather(up_projection_bias, "fsdp", axis=0, tiled=True),
        lax.all_gather(down_projection_weight, "fsdp", axis=0, tiled=True),
        lax.all_gather(down_projection_bias, "fsdp", axis=0, tiled=True),
    )
    seqs_here, block_rows, feature_count = hidden_in.shape
    row_count = seqs_here * block_rows
    hidden = hidden_in.astype(jnp.float32).reshape(row_count, feature_count)
    normed_input, attn_back = jax.vjp(
        layer_norm, hidden, attn_gain_all.astype(jnp.float32), attn_shift_all.astype(jnp.float32)
    )
    normed_low = normed_input.astype(jnp.bfloat16)
    joined_heads = jnp.dot(normed_low, qkv_weight_all, preferred_element_type=jnp.float32)
    queries = (
        (joined_heads[:, :feature_count] + query_bias_all.astype(jnp.float32)) * 0.125
    ).astype(jnp.bfloat16)
    key_rows = joined_heads[:, feature_count : 2 * feature_count].astype(jnp.bfloat16)
    values = (joined_heads[:, 2 * feature_count :] + value_bias_all.astype(jnp.float32)).astype(
        jnp.bfloat16
    )
    query_heads = queries.reshape(seqs_here, block_rows, HEADS, HD)
    keys_seq = key_rows.reshape(seqs_here, block_rows, feature_count)
    values_seq = values.reshape(seqs_here, block_rows, feature_count)
    query_pos = lax.axis_index("ctx") * block_rows + jnp.arange(block_rows)
    start_state = (
        jnp.full((seqs_here, HEADS, block_rows), NEG_BIG, jnp.float32),
        jnp.zeros((seqs_here, HEADS, block_rows), jnp.float32),
        jnp.zeros((seqs_here, HEADS, block_rows, HD), jnp.float32),
    )
    forward_step = partial(forward_block, queries=query_heads, query_pos=query_pos)
    keys_all, values_all = (
        lax.all_gather(keys_seq, "ctx", axis=1, tiled=True),
        lax.all_gather(values_seq, "ctx", axis=1, tiled=True),
    )
    run_max, run_sum, accumulated = sweep_blocks(
        start_state, (keys_all, values_all), 0, block_rows, forward_step
    )
    row_stats = run_max + jnp.log(run_sum)
    attended_rows = accumulated / run_sum[..., None]
    attended_low = (
        jnp.transpose(attended_rows, (0, 2, 1, 3))
        .reshape(row_count, feature_count)
        .astype(jnp.bfloat16)
    )
    middle_residual = (
        hidden
        + jnp.dot(attended_low, proj_weight_all, preferred_element_type=jnp.float32)
        + proj_bias_all.astype(jnp.float32)
    )
    second_normed, mlp_back = jax.vjp(
        layer_norm,
        middle_residual,
        mlp_gain_all.astype(jnp.float32),
        mlp_shift_all.astype(jnp.float32),
    )
    second_low = second_normed.astype(jnp.bfloat16)
    inner_preactivation = jnp.dot(
        second_low, up_weight_all, preferred_element_type=jnp.float32
    ) + up_bias_all.astype(jnp.float32)
    active_hidden, gelu_back = jax.vjp(exact_gelu, inner_preactivation)
    active_low = active_hidden.astype(jnp.bfloat16)
    block_result = (
        middle_residual
        + jnp.dot(active_low, down_weight_all, preferred_element_type=jnp.float32)
        + down_bias_all.astype(jnp.float32)
    )
    block_out = block_result.astype(jnp.bfloat16).reshape(seqs_here, block_rows, feature_count)
    qkv_back, proj_back, up_back, down_back = (
        lax.all_gather(query_key_value_weight, "fsdp", axis=0, tiled=True),
        lax.all_gather(projection_output_weight, "fsdp", axis=0, tiled=True),
        lax.all_gather(up_projection_weight, "fsdp", axis=0, tiled=True),
        lax.all_gather(down_projection_weight, "fsdp", axis=0, tiled=True),
    )
    grad_top = out_grad.astype(jnp.float32).reshape(row_count, feature_count)
    branch_down = grad_top.astype(jnp.bfloat16)
    down_grad = jnp.einsum("rf,rd->fd", active_low, branch_down, preferred_element_type=jnp.float32)
    down_bias_grad = jnp.sum(branch_down, axis=0, dtype=jnp.float32)
    grad_active = jnp.einsum(
        "rd,fd->rf", branch_down, down_back, preferred_element_type=jnp.float32
    )
    inner_grad = gelu_back(grad_active)[0].astype(jnp.bfloat16)
    up_grad = jnp.einsum("rd,rf->df", second_low, inner_grad, preferred_element_type=jnp.float32)
    up_bias_grad = jnp.sum(inner_grad, axis=0, dtype=jnp.float32)
    grad_second = jnp.einsum("rf,df->rd", inner_grad, up_back, preferred_element_type=jnp.float32)
    grad_middle, mlp_gain_grad, mlp_shift_grad = mlp_back(grad_second)
    grad_middle = grad_middle + grad_top
    branch_up = grad_middle.astype(jnp.bfloat16)
    proj_grad = jnp.einsum("rd,re->de", attended_low, branch_up, preferred_element_type=jnp.float32)
    proj_bias_grad = jnp.sum(branch_up, axis=0, dtype=jnp.float32)
    att_grad = jnp.einsum(
        "re,de->rd", branch_up, proj_back, preferred_element_type=jnp.float32
    ).astype(jnp.bfloat16)
    grad_heads = att_grad.reshape(seqs_here, block_rows, HEADS, HD)
    row_delta = jnp.sum(
        attended_rows * jnp.transpose(grad_heads, (0, 2, 1, 3)).astype(jnp.float32), axis=-1
    )
    query_zero = jnp.zeros((seqs_here, HEADS, block_rows, HD), jnp.float32)
    back_state = (query_zero,)
    backward_step = partial(
        query_block,
        queries=query_heads,
        grad_out=grad_heads,
        row_stats=row_stats,
        row_delta=row_delta,
        query_pos=query_pos,
    )
    back_result = sweep_blocks(back_state, (keys_all, values_all), 0, block_rows, backward_step)
    query_grad = back_result[0]
    stats_all, delta_all = (
        lax.all_gather(
            jnp.transpose(row_stats, (0, 2, 1)).astype(jnp.bfloat16), "ctx", axis=1, tiled=True
        ).astype(jnp.float32),
        lax.all_gather(
            jnp.transpose(row_delta, (0, 2, 1)).astype(jnp.bfloat16), "ctx", axis=1, tiled=True
        ).astype(jnp.float32),
    )
    own_keys = split_heads(keys_seq)
    own_values = split_heads(values_seq)

    def key_step(carry_state, blocks, query_start):
        stats_blk = lax.dynamic_slice_in_dim(stats_all, query_start, block_rows, 1)
        delta_blk = lax.dynamic_slice_in_dim(delta_all, query_start, block_rows, 1)
        return key_block(
            carry_state,
            blocks[0],
            blocks[1],
            stats_blk,
            delta_blk,
            query_start,
            own_keys,
            own_values,
            query_pos,
        )

    key_zero = jnp.zeros((seqs_here, block_rows, HEADS, HD), jnp.float32)
    key_grad_own, value_grad_own = sweep_blocks(
        (key_zero, key_zero),
        (
            lax.all_gather(query_heads, "ctx", axis=1, tiled=True),
            lax.all_gather(grad_heads, "ctx", axis=1, tiled=True),
        ),
        jnp.int32(0),
        block_rows,
        key_step,
    )
    key_grad_sum = key_grad_own.reshape(seqs_here, block_rows, feature_count)
    value_grad_sum = value_grad_own.reshape(seqs_here, block_rows, feature_count)
    query_grad_low = (
        jnp.transpose(query_grad, (0, 2, 1, 3))
        .reshape(row_count, feature_count)
        .astype(jnp.bfloat16)
    )
    key_grad_low = key_grad_sum.reshape(row_count, feature_count).astype(jnp.bfloat16)
    value_grad_low = value_grad_sum.reshape(row_count, feature_count).astype(jnp.bfloat16)
    joined_grad = jnp.concatenate(
        [
            (query_grad_low.astype(jnp.float32) * 0.125).astype(jnp.bfloat16),
            key_grad_low,
            value_grad_low,
        ],
        axis=1,
    )
    qkv_grad = jnp.einsum("rd,rf->df", normed_low, joined_grad, preferred_element_type=jnp.float32)
    query_bias_grad = jnp.sum(query_grad_low, axis=0, dtype=jnp.float32) * 0.125
    value_bias_grad = jnp.sum(value_grad_low, axis=0, dtype=jnp.float32)
    grad_normed = jnp.einsum("rf,df->rd", joined_grad, qkv_back, preferred_element_type=jnp.float32)
    grad_hidden, attn_gain_grad, attn_shift_grad = attn_back(grad_normed)
    input_grad = (
        (grad_middle + grad_hidden)
        .astype(jnp.bfloat16)
        .reshape(seqs_here, block_rows, feature_count)
    )
    summed = (
        lax.psum_scatter(
            attn_gain_grad.astype(jnp.bfloat16), "fsdp", scatter_dimension=0, tiled=True
        ).astype(jnp.float32),
        lax.psum_scatter(
            attn_shift_grad.astype(jnp.bfloat16), "fsdp", scatter_dimension=0, tiled=True
        ).astype(jnp.float32),
        lax.psum_scatter(
            qkv_grad.astype(jnp.bfloat16), "fsdp", scatter_dimension=0, tiled=True
        ).astype(jnp.float32),
        lax.psum_scatter(
            query_bias_grad.astype(jnp.bfloat16), "fsdp", scatter_dimension=0, tiled=True
        ).astype(jnp.float32),
        lax.psum_scatter(
            value_bias_grad.astype(jnp.bfloat16), "fsdp", scatter_dimension=0, tiled=True
        ).astype(jnp.float32),
        lax.psum_scatter(
            proj_grad.astype(jnp.bfloat16), "fsdp", scatter_dimension=0, tiled=True
        ).astype(jnp.float32),
        lax.psum_scatter(
            proj_bias_grad.astype(jnp.bfloat16), "fsdp", scatter_dimension=0, tiled=True
        ).astype(jnp.float32),
        lax.psum_scatter(
            mlp_gain_grad.astype(jnp.bfloat16), "fsdp", scatter_dimension=0, tiled=True
        ).astype(jnp.float32),
        lax.psum_scatter(
            mlp_shift_grad.astype(jnp.bfloat16), "fsdp", scatter_dimension=0, tiled=True
        ).astype(jnp.float32),
        lax.psum_scatter(
            up_grad.astype(jnp.bfloat16), "fsdp", scatter_dimension=0, tiled=True
        ).astype(jnp.float32),
        lax.psum_scatter(
            up_bias_grad.astype(jnp.bfloat16), "fsdp", scatter_dimension=0, tiled=True
        ).astype(jnp.float32),
        lax.psum_scatter(
            down_grad.astype(jnp.bfloat16), "fsdp", scatter_dimension=0, tiled=True
        ).astype(jnp.float32),
        lax.psum_scatter(
            down_bias_grad.astype(jnp.bfloat16), "fsdp", scatter_dimension=0, tiled=True
        ).astype(jnp.float32),
    )
    summed = jax.tree.map(
        lambda part: part.astype(jnp.float32), lax.psum(as_sent(tuple(summed)), "ctx")
    )
    return (block_out, input_grad) + tuple(summed) + (row_stats,)


ROWS = 256


def low(value):
    return value.astype(jnp.bfloat16)


def wide(value):
    return value.astype(jnp.float32)


def dot(a, b):
    return jnp.dot(a, b, preferred_element_type=jnp.float32)


def xor_send(value, axis, bit, count):
    return lax.ppermute(value, axis, [(i, i ^ bit) for i in range(count)])


def shift_send(value, steps, count):
    return lax.ppermute(value, "ctx", [(i, (i + steps) % count) for i in range(count)])


def gather_fsdp(piece):
    me = lax.axis_index("fsdp")
    rows = piece.shape[0]
    half = rows // 2
    by_x = xor_send(piece, "fsdp", 2, 8)
    by_y = xor_send(piece, "fsdp", 4, 8)
    corner_top = xor_send(by_x[:half], "fsdp", 4, 8)
    corner_low = xor_send(by_y[half:], "fsdp", 2, 8)
    parts = [(0, 0, piece), (2, 0, by_x), (4, 0, by_y), (6, 0, corner_top), (6, half, corner_low)]
    whole = jnp.zeros((8 * rows,) + piece.shape[1:], piece.dtype)
    for place, offset, part in parts:
        other = xor_send(part, "fsdp", 1, 8)
        start = jnp.bitwise_xor(me, place) * rows + offset
        whole = lax.dynamic_update_slice_in_dim(whole, part, start, 0)
        start = jnp.bitwise_xor(me, place + 1) * rows + offset
        whole = lax.dynamic_update_slice_in_dim(whole, other, start, 0)
    return whole


def scatter_fsdp(grad):
    me = lax.axis_index("fsdp")
    core, x, y = me % 2, (me // 2) % 2, me // 4
    rows, columns = grad.shape
    blocks = grad.reshape(2, 2, 2, rows // 8, columns)
    kept = lax.dynamic_index_in_dim(blocks, core, 2, keepdims=False)
    sent = low(lax.dynamic_index_in_dim(blocks, 1 - core, 2, keepdims=False))
    total = low(wide(kept) + wide(xor_send(sent, "fsdp", 1, 8)))
    half = rows // 16
    top, bottom = total[:, :, :half], total[:, :, half:]

    def fold(part, axis, place, bit):
        keep = lax.dynamic_index_in_dim(part, place, axis, keepdims=False)
        send = lax.dynamic_index_in_dim(part, 1 - place, axis, keepdims=False)
        return low(wide(keep) + wide(xor_send(send, "fsdp", bit, 8)))

    top = fold(fold(top, 1, x, 2), 0, y, 4)
    bottom = fold(fold(bottom, 0, y, 4), 0, x, 2)
    return jnp.concatenate([top, bottom], axis=0)


def sum_ctx(part):
    me = lax.axis_index("ctx")
    odd = me % 2
    rows = part.shape[0]
    halves = part.reshape((2, rows // 2) + part.shape[1:])
    keep = lax.dynamic_index_in_dim(halves, odd, 0, keepdims=False)
    send = lax.dynamic_index_in_dim(halves, 1 - odd, 0, keepdims=False)
    own = low(wide(keep) + wide(xor_send(send, "ctx", 1, 4)))
    own = low(wide(own) + wide(xor_send(own, "ctx", 2, 4)))
    other = xor_send(own, "ctx", 1, 4)
    return jnp.where(odd == 0, jnp.concatenate([own, other]), jnp.concatenate([other, own]))


def gather_ctx(block):
    me = lax.axis_index("ctx")
    whole = jnp.zeros((4,) + block.shape, block.dtype)
    whole = lax.dynamic_update_index_in_dim(whole, block, me, 0)
    right = left = block
    for step in range(1, 4):
        right = lax.ppermute(right, "ctx", [(i, i + 1) for i in range(step - 1, 3)])
        left = lax.ppermute(left, "ctx", [(i, i - 1) for i in range(1, 5 - step)])
        source = (me - step) % 4
        other = (me + step) % 4
        whole = lax.dynamic_update_index_in_dim(
            whole,
            jnp.where(me >= step, right, lax.dynamic_index_in_dim(whole, source, 0, keepdims=False)),
            source,
            0,
        )
        whole = lax.dynamic_update_index_in_dim(
            whole,
            jnp.where(me + step < 4, left, lax.dynamic_index_in_dim(whole, other, 0, keepdims=False)),
            other,
            0,
        )
    return whole.reshape((-1,) + block.shape[1:])


def scatter_ctx(total):
    me = lax.axis_index("ctx")

    def block(index):
        return lax.dynamic_index_in_dim(total, jnp.clip(index, 0, 3), 0, keepdims=False)

    right = left = None
    for step in range(3):
        going_right, going_left = block(3 - step + me), block(step - 3 + me)
        if step:
            going_right = wide(going_right) + wide(right)
            going_left = wide(going_left) + wide(left)
        right = lax.ppermute(low(going_right), "ctx", [(i, i + 1) for i in range(step + 1)])
        left = lax.ppermute(low(going_left), "ctx", [(i, i - 1) for i in range(3 - step, 4)])
    return wide(block(me)) + wide(right) + wide(left)


def heads_to_positions(value, ordered_axis):
    me = lax.axis_index("ctx")
    result = jnp.zeros(value.shape, value.dtype)
    result = lax.dynamic_update_index_in_dim(
        result, lax.dynamic_index_in_dim(value, me, 0, keepdims=False), me, 0
    )
    for step in (2, 1, 3):
        piece = lax.dynamic_index_in_dim(value, (me + step) % 4, 0, keepdims=False)
        result = lax.dynamic_update_index_in_dim(
            result, shift_send(piece, step, 4), (me - step) % 4, 0
        )
    return jnp.moveaxis(result, 0, ordered_axis)


def masked_scores(keys, queries_t, tile):
    scores = dot(keys, queries_t)
    key_pos = lax.broadcasted_iota(jnp.int32, (ROWS, ROWS), 0)
    query_pos = lax.broadcasted_iota(jnp.int32, (ROWS, ROWS), 1)
    diagonal = jnp.where(key_pos <= query_pos, scores[tile * ROWS :], NEG_BIG)
    if tile == 0:
        return diagonal
    return jnp.concatenate([scores[: tile * ROWS], diagonal], axis=0)


def attend_kernel(qkv_ref, out_ref, stats_ref):
    length, width = out_ref.shape
    heads = width // HD
    queries_t = qkv_ref[:, :width].T
    values_t = qkv_ref[:, 2 * width :].T
    for head in range(heads):
        keys = qkv_ref[:, width + head * HD : width + (head + 1) * HD]
        lanes = slice(head * HD, (head + 1) * HD)
        for tile in range(length // ROWS):
            rows = slice(tile * ROWS, (tile + 1) * ROWS)
            seen = (tile + 1) * ROWS
            scores = masked_scores(keys[:seen], queries_t[lanes, rows], tile)
            top = jnp.max(scores, axis=0, keepdims=True)
            weights = jnp.exp(scores - top)
            total = jnp.sum(weights, axis=0, keepdims=True)
            mixed = dot(values_t[lanes, :seen], low(weights)) / total
            out_ref[rows, lanes] = mixed.T
            stats_ref[head : head + 1, rows] = top + jnp.log(total)


def attend_back_kernel(qkv_ref, att_ref, grad_ref, stats_ref, out_ref, key_ref, value_ref):
    length, width = att_ref.shape
    heads = width // HD
    queries_t = qkv_ref[:, :width].T
    keys_t = qkv_ref[:, width : 2 * width].T
    grad_t = grad_ref[...].T
    product_t = (att_ref[...] * wide(grad_ref[...])).T
    for head in range(heads):
        lanes = slice(head * HD, (head + 1) * HD)
        queries = qkv_ref[:, head * HD : (head + 1) * HD]
        keys = qkv_ref[:, width + head * HD : width + (head + 1) * HD]
        values = qkv_ref[:, 2 * width + head * HD : 2 * width + (head + 1) * HD]
        grads = grad_ref[:, lanes]
        delta = jnp.sum(product_t[lanes], axis=0, keepdims=True)
        key_ref[...] = jnp.zeros_like(key_ref)
        value_ref[...] = jnp.zeros_like(value_ref)
        for tile in range(length // ROWS):
            rows = slice(tile * ROWS, (tile + 1) * ROWS)
            seen = (tile + 1) * ROWS
            scores = masked_scores(keys[:seen], queries_t[lanes, rows], tile)
            prob = jnp.exp(scores - stats_ref[head : head + 1, rows])
            prob_grad = dot(values[:seen], grad_t[lanes, rows])
            score_grad = low(prob * (prob_grad - delta[:, rows]))
            query_grad = dot(keys_t[lanes, :seen], score_grad)
            out_ref[rows, lanes] = low(low(query_grad).T * jnp.bfloat16(0.125))
            key_ref[:seen] += dot(score_grad, queries[rows])
            value_ref[:seen] += dot(low(prob), grads[rows])
        out_ref[:, width + head * HD : width + (head + 1) * HD] = low(key_ref[...])
        out_ref[:, 2 * width + head * HD : 2 * width + (head + 1) * HD] = low(value_ref[...])


def attend(qkv):
    length, width = qkv.shape[0], qkv.shape[1] // 3
    return pl.pallas_call(
        attend_kernel,
        out_shape=(
            jax.ShapeDtypeStruct((length, width), jnp.float32),
            jax.ShapeDtypeStruct((width // HD, length), jnp.float32),
        ),
        compiler_params=pltpu.CompilerParams(vmem_limit_bytes=40 * 1024 * 1024),
        cost_estimate=pl.CostEstimate(
            flops=8 * length * length * width, bytes_accessed=4 * length * width * 4, transcendentals=2 * length * length
        ),
    )(qkv)


def attend_back(qkv, attended, grads, stats):
    length, width = attended.shape
    return pl.pallas_call(
        attend_back_kernel,
        out_shape=jax.ShapeDtypeStruct((length, 3 * width), jnp.bfloat16),
        scratch_shapes=[pltpu.VMEM((length, HD), jnp.float32), pltpu.VMEM((length, HD), jnp.float32)],
        compiler_params=pltpu.CompilerParams(vmem_limit_bytes=40 * 1024 * 1024),
        cost_estimate=pl.CostEstimate(
            flops=20 * length * length * width, bytes_accessed=5 * length * width * 4, transcendentals=2 * length * length
        ),
    )(qkv, attended, grads, stats)


def norm_parts(values):
    center = values - jnp.mean(values, axis=-1, keepdims=True)
    inverse = lax.rsqrt(jnp.mean(center * center, axis=-1, keepdims=True) + 1e-05)
    return center * inverse, inverse


def norm_back(grad, unit, inverse, gain):
    inner = grad * gain
    mean_inner = jnp.mean(inner, axis=-1, keepdims=True)
    mean_product = jnp.mean(inner * unit, axis=-1, keepdims=True)
    return (
        inverse * (inner - mean_inner - unit * mean_product),
        jnp.sum(grad * unit, axis=0),
        jnp.sum(grad, axis=0),
    )


def local_fast(
    hidden_in,
    attn_gain,
    attn_shift,
    query_key_value_weight,
    query_bias,
    value_bias,
    projection_output_weight,
    projection_output_bias,
    mlp_gain,
    mlp_shift,
    up_projection_weight,
    up_projection_bias,
    down_projection_weight,
    down_projection_bias,
    out_grad,
):
    seqs, block_rows, width = hidden_in.shape
    place = lax.axis_index("ctx")
    share = width // 4
    row_count = seqs * block_rows
    shard = width // 8

    vectors = jnp.stack(
        [attn_gain, attn_shift, query_bias, value_bias, projection_output_bias, mlp_gain, mlp_shift, down_projection_bias]
        + list(up_projection_bias.reshape(4, shard))
        + [attn_gain] * 4
    )
    vectors_all = wide(gather_fsdp(vectors)).reshape(8, 16, shard)
    (gain_1, shift_1, bias_q, bias_v, bias_proj, gain_2, shift_2, bias_down) = (
        vectors_all[:, i].reshape(width) for i in range(8)
    )
    bias_up = vectors_all[:, 8:12].reshape(4 * width)

    def heads_here(array):
        return lax.dynamic_slice_in_dim(array, place * share, share, array.ndim - 1)

    qkv_own = heads_here(query_key_value_weight.reshape(shard, 3, width)).reshape(shard, 3 * share)
    qkv_all = gather_fsdp(qkv_own)
    full = [gather_ctx(hidden_in[s]) for s in range(seqs)]
    proj_all = gather_fsdp(projection_output_weight)
    up_all = gather_fsdp(up_projection_weight)
    down_all = gather_fsdp(down_projection_weight)

    bias_qkv = jnp.concatenate([heads_here(bias_q), jnp.zeros((share,), jnp.float32), heads_here(bias_v)])
    scale = jnp.concatenate([jnp.full((share,), 0.125, jnp.float32), jnp.ones((2 * share,), jnp.float32)])
    normed, qkv, attended, stats, gathered = [], [], [], [], []
    for s in range(seqs):
        unit, unused = norm_parts(wide(full[s]))
        normed.append(low(unit * gain_1 + shift_1))
        qkv.append(low((dot(normed[s], qkv_all) + bias_qkv) * scale))
        att, stat = attend(qkv[s])
        attended.append(att)
        stats.append(stat)
        gathered.append(heads_to_positions(low(att).reshape(4, block_rows, share), 1).reshape(block_rows, width))
    stats_all = jnp.stack(stats)
    heads_each = stats_all.shape[1]
    stats_out = heads_to_positions(
        jnp.moveaxis(stats_all.reshape(seqs, heads_each, 4, block_rows), 2, 0), 1
    ).reshape(seqs, 4 * heads_each, block_rows)
    attended_low = jnp.concatenate(gathered)

    hidden = wide(hidden_in).reshape(row_count, width)
    middle = hidden + dot(attended_low, proj_all) + bias_proj
    unit_2, inverse_2 = norm_parts(middle)
    second = low(unit_2 * gain_2 + shift_2)
    inner = dot(second, up_all) + bias_up
    below = 0.5 * (1.0 + lax.erf(inner * 0.7071067811865476))
    active = low(inner * below)
    slope = below + inner * (jnp.exp(-0.5 * inner * inner) * 0.3989422804014327)
    block_out = low(middle + dot(active, down_all) + bias_down).reshape(seqs, block_rows, width)

    branch_down = out_grad.reshape(row_count, width)
    top = wide(branch_down)
    contract_rows = (((0,), (0,)), ((), ()))
    contract_columns = (((1,), (1,)), ((), ()))

    def weight_grad(a, b):
        return lax.dot_general(a, b, contract_rows, preferred_element_type=jnp.float32)

    def through(a, b):
        return lax.dot_general(a, b, contract_columns, preferred_element_type=jnp.float32)

    down_grad = sum_ctx(scatter_fsdp(low(weight_grad(active, branch_down))))
    inner_grad = low(through(branch_down, down_all) * slope)
    up_grad = sum_ctx(scatter_fsdp(low(weight_grad(second, inner_grad))))
    grad_middle, gain_2_grad, shift_2_grad = norm_back(through(inner_grad, up_all), unit_2, inverse_2, gain_2)
    grad_middle = grad_middle + top
    branch_up = low(grad_middle)
    att_grad = low(through(branch_up, proj_all))
    proj_grad = sum_ctx(scatter_fsdp(low(weight_grad(attended_low, branch_up))))

    att_grad = jnp.moveaxis(att_grad.reshape(seqs, block_rows, 4, share), 2, 1)
    joined, own_grads = [], []
    qkv_grad = 0.0
    for s in range(seqs):
        grads = heads_to_positions(att_grad[s], 0).reshape(4 * block_rows, share)
        joined.append(attend_back(qkv[s], attended[s], grads, stats[s]))
        partial_normed = low(through(joined[s], qkv_all)).reshape(4, block_rows, width)
        own_grads.append(scatter_ctx(partial_normed))
        qkv_grad = qkv_grad + weight_grad(normed[s], joined[s])
    qkv_part = scatter_fsdp(low(qkv_grad))
    pieces = jnp.zeros((4,) + qkv_part.shape, qkv_part.dtype)
    pieces = lax.dynamic_update_index_in_dim(pieces, qkv_part, place, 0)
    for step in (2, 1, 3):
        pieces = lax.dynamic_update_index_in_dim(pieces, shift_send(qkv_part, step, 4), (place - step) % 4, 0)
    qkv_out = wide(jnp.moveaxis(pieces.reshape(4, shard, 3, share), 0, 2).reshape(shard, 3 * width))

    joined_all = jnp.concatenate(joined)
    bias_sums = jnp.sum(joined_all, axis=0, dtype=jnp.float32)
    zero_row = jnp.zeros((width,), jnp.float32)
    query_bias_grad = lax.dynamic_update_slice_in_dim(zero_row, bias_sums[:share], place * share, 0)
    value_bias_grad = lax.dynamic_update_slice_in_dim(zero_row, bias_sums[2 * share :], place * share, 0)

    unit_1, inverse_1 = norm_parts(hidden)
    grad_hidden, gain_1_grad, shift_1_grad = norm_back(jnp.concatenate(own_grads), unit_1, inverse_1, gain_1)
    input_grad = low(grad_middle + grad_hidden).reshape(seqs, block_rows, width)

    rows = [
        gain_1_grad,
        shift_1_grad,
        query_bias_grad,
        value_bias_grad,
        jnp.sum(branch_up, axis=0, dtype=jnp.float32),
        gain_2_grad,
        shift_2_grad,
        jnp.sum(branch_down, axis=0, dtype=jnp.float32),
    ]
    up_bias_grad = jnp.sum(inner_grad, axis=0, dtype=jnp.float32)
    small = jnp.concatenate(
        [
            jnp.stack(rows).reshape(8, 8, shard).transpose(1, 0, 2),
            up_bias_grad.reshape(8, 4, shard),
            jnp.zeros((8, 4, shard), jnp.float32),
        ],
        axis=1,
    )
    small = wide(sum_ctx(scatter_fsdp(low(small.reshape(8 * 16, shard)))))
    return (
        block_out,
        input_grad,
        small[0],
        small[1],
        qkv_out,
        small[2],
        small[3],
        wide(proj_grad),
        small[4],
        small[5],
        small[6],
        wide(up_grad),
        small[8:12].reshape(4 * shard),
        wide(down_grad),
        small[7],
        stats_out,
    )


def solution(mesh):
    fast = mesh.shape["ctx"] == 4 and mesh.shape["fsdp"] == 8
    chosen = local_fast if fast else local_general
    placed = (
        P("fsdp", "ctx", None),
        P("fsdp"),
        P("fsdp"),
        P("fsdp", None),
        P("fsdp"),
        P("fsdp"),
        P("fsdp", None),
        P("fsdp"),
        P("fsdp"),
        P("fsdp"),
        P("fsdp", None),
        P("fsdp"),
        P("fsdp", None),
        P("fsdp"),
        P("fsdp", "ctx", None),
    )
    return jax.shard_map(
        chosen,
        mesh=mesh,
        in_specs=placed,
        out_specs=(
            P("fsdp", "ctx", None),
            P("fsdp", "ctx", None),
            P("fsdp"),
            P("fsdp"),
            P("fsdp", None),
            P("fsdp"),
            P("fsdp"),
            P("fsdp", None),
            P("fsdp"),
            P("fsdp"),
            P("fsdp"),
            P("fsdp", None),
            P("fsdp"),
            P("fsdp", None),
            P("fsdp"),
            P("fsdp", None, "ctx"),
        ),
        check_vma=False,
    )
```

```python
from functools import partial

import jax
import jax.numpy as jnp
from jax import lax
from jax.experimental import pallas as pl
from jax.experimental.pallas import tpu as pltpu
from jax.sharding import PartitionSpec as P

HEADS = 12
HD = 64


NEG_BIG = -1e30


def as_sent(value):
    return jax.tree.map(lambda a: a.astype(jnp.bfloat16) if a.dtype == jnp.float32 else a, value)


def layer_norm(values, gain, shift):
    center = values - jnp.mean(values, axis=-1, keepdims=True)
    spread = jnp.mean(center * center, axis=-1, keepdims=True)
    return center * lax.rsqrt(spread + 1e-05) * gain + shift


def exact_gelu(values):
    return jax.nn.gelu(values, approximate=False)


def split_heads(values):
    return values.reshape(values.shape[0], values.shape[1], HEADS, HD)


def forward_block(carry_state, blocks, key_start, queries, query_pos):
    keys_blk, values_blk = blocks

    def forward_update(unused):
        run_max, run_sum, accumulated = carry_state
        scores = jnp.einsum(
            "sbhe,snhe->shbn", queries, split_heads(keys_blk), preferred_element_type=jnp.float32
        )
        key_pos = key_start + jnp.arange(keys_blk.shape[1])
        visible = query_pos[:, None] >= key_pos[None, :]
        scores = jnp.where(visible, scores, NEG_BIG)
        new_max = jnp.maximum(run_max, jnp.max(scores, axis=-1))
        weights = jnp.where(visible, jnp.exp(scores - new_max[..., None]), 0.0)
        factor = jnp.exp(run_max - new_max)
        new_sum = run_sum * factor + jnp.sum(weights, axis=-1)
        new_acc = accumulated * factor[..., None] + jnp.einsum(
            "shbn,snhe->shbe",
            weights.astype(jnp.bfloat16),
            split_heads(values_blk),
            preferred_element_type=jnp.float32,
        )
        return (new_max, new_sum, new_acc)

    return lax.cond(key_start > query_pos[-1], lambda unused: carry_state, forward_update, None)


def query_block(carry_state, blocks, key_start, queries, grad_out, row_stats, row_delta, query_pos):
    keys_blk, values_blk = blocks

    def query_update(unused):
        query_grad = carry_state[0]
        key_heads = split_heads(keys_blk)
        scores = jnp.einsum(
            "sbhe,snhe->shbn", queries, key_heads, preferred_element_type=jnp.float32
        )
        key_pos = key_start + jnp.arange(keys_blk.shape[1])
        visible = query_pos[:, None] >= key_pos[None, :]
        probability = jnp.where(visible, jnp.exp(scores - row_stats[..., None]), 0.0)
        prob_grad = jnp.einsum(
            "sbhe,snhe->shbn", grad_out, split_heads(values_blk), preferred_element_type=jnp.float32
        )
        score_grad = (probability * (prob_grad - row_delta[..., None])).astype(jnp.bfloat16)
        return (
            query_grad
            + jnp.einsum(
                "shbn,snhe->shbe", score_grad, key_heads, preferred_element_type=jnp.float32
            ),
        )

    return lax.cond(key_start > query_pos[-1], lambda unused: carry_state, query_update, None)


def key_block(
    carry_state,
    query_blk,
    grad_blk,
    stats_blk,
    delta_blk,
    query_start,
    key_heads,
    value_heads,
    key_pos,
):
    query_pos = query_start + jnp.arange(query_blk.shape[1])

    def key_update(unused):
        key_grad, value_grad = carry_state
        stats_now = jnp.transpose(stats_blk, (0, 2, 1))
        delta_now = jnp.transpose(delta_blk, (0, 2, 1))
        scores = jnp.einsum(
            "sbhe,snhe->shbn", query_blk, key_heads, preferred_element_type=jnp.float32
        )
        visible = query_pos[:, None] >= key_pos[None, :]
        probability = jnp.where(visible, jnp.exp(scores - stats_now[..., None]), 0.0)
        value_grad = value_grad + jnp.einsum(
            "shbn,sbhe->snhe",
            probability.astype(jnp.bfloat16),
            grad_blk,
            preferred_element_type=jnp.float32,
        )
        prob_grad = jnp.einsum(
            "sbhe,snhe->shbn", grad_blk, value_heads, preferred_element_type=jnp.float32
        )
        score_grad = (probability * (prob_grad - delta_now[..., None])).astype(jnp.bfloat16)
        key_grad = key_grad + jnp.einsum(
            "shbn,sbhe->snhe", score_grad, query_blk, preferred_element_type=jnp.float32
        )
        return (key_grad, value_grad)

    return lax.cond(query_pos[-1] < key_pos[0], lambda unused: carry_state, key_update, None)


def sweep_blocks(carry_state, arrays, first_row, block_rows, step):
    block_count = arrays[0].shape[1] // block_rows

    def one_block(block_num, carry):
        offset = block_num * block_rows
        blocks = tuple((lax.dynamic_slice_in_dim(array, offset, block_rows, 1) for array in arrays))
        return step(carry, blocks, first_row + offset)

    return lax.fori_loop(0, block_count, one_block, carry_state)


def local_general(
    hidden_in,
    attn_gain,
    attn_shift,
    query_key_value_weight,
    query_bias,
    value_bias,
    projection_output_weight,
    projection_output_bias,
    mlp_gain,
    mlp_shift,
    up_projection_weight,
    up_projection_bias,
    down_projection_weight,
    down_projection_bias,
    out_grad,
):
    (
        attn_gain_all,
        attn_shift_all,
        qkv_weight_all,
        query_bias_all,
        value_bias_all,
        proj_weight_all,
        proj_bias_all,
        mlp_gain_all,
        mlp_shift_all,
        up_weight_all,
        up_bias_all,
        down_weight_all,
        down_bias_all,
    ) = (
        lax.all_gather(attn_gain, "fsdp", axis=0, tiled=True),
        lax.all_gather(attn_shift, "fsdp", axis=0, tiled=True),
        lax.all_gather(query_key_value_weight, "fsdp", axis=0, tiled=True),
        lax.all_gather(query_bias, "fsdp", axis=0, tiled=True),
        lax.all_gather(value_bias, "fsdp", axis=0, tiled=True),
        lax.all_gather(projection_output_weight, "fsdp", axis=0, tiled=True),
        lax.all_gather(projection_output_bias, "fsdp", axis=0, tiled=True),
        lax.all_gather(mlp_gain, "fsdp", axis=0, tiled=True),
        lax.all_gather(mlp_shift, "fsdp", axis=0, tiled=True),
        lax.all_gather(up_projection_weight, "fsdp", axis=0, tiled=True),
        lax.all_gather(up_projection_bias, "fsdp", axis=0, tiled=True),
        lax.all_gather(down_projection_weight, "fsdp", axis=0, tiled=True),
        lax.all_gather(down_projection_bias, "fsdp", axis=0, tiled=True),
    )
    seqs_here, block_rows, feature_count = hidden_in.shape
    row_count = seqs_here * block_rows
    hidden = hidden_in.astype(jnp.float32).reshape(row_count, feature_count)
    normed_input, attn_back = jax.vjp(
        layer_norm, hidden, attn_gain_all.astype(jnp.float32), attn_shift_all.astype(jnp.float32)
    )
    normed_low = normed_input.astype(jnp.bfloat16)
    joined_heads = jnp.dot(normed_low, qkv_weight_all, preferred_element_type=jnp.float32)
    queries = (
        (joined_heads[:, :feature_count] + query_bias_all.astype(jnp.float32)) * 0.125
    ).astype(jnp.bfloat16)
    key_rows = joined_heads[:, feature_count : 2 * feature_count].astype(jnp.bfloat16)
    values = (joined_heads[:, 2 * feature_count :] + value_bias_all.astype(jnp.float32)).astype(
        jnp.bfloat16
    )
    query_heads = queries.reshape(seqs_here, block_rows, HEADS, HD)
    keys_seq = key_rows.reshape(seqs_here, block_rows, feature_count)
    values_seq = values.reshape(seqs_here, block_rows, feature_count)
    query_pos = lax.axis_index("ctx") * block_rows + jnp.arange(block_rows)
    start_state = (
        jnp.full((seqs_here, HEADS, block_rows), NEG_BIG, jnp.float32),
        jnp.zeros((seqs_here, HEADS, block_rows), jnp.float32),
        jnp.zeros((seqs_here, HEADS, block_rows, HD), jnp.float32),
    )
    forward_step = partial(forward_block, queries=query_heads, query_pos=query_pos)
    keys_all, values_all = (
        lax.all_gather(keys_seq, "ctx", axis=1, tiled=True),
        lax.all_gather(values_seq, "ctx", axis=1, tiled=True),
    )
    run_max, run_sum, accumulated = sweep_blocks(
        start_state, (keys_all, values_all), 0, block_rows, forward_step
    )
    row_stats = run_max + jnp.log(run_sum)
    attended_rows = accumulated / run_sum[..., None]
    attended_low = (
        jnp.transpose(attended_rows, (0, 2, 1, 3))
        .reshape(row_count, feature_count)
        .astype(jnp.bfloat16)
    )
    middle_residual = (
        hidden
        + jnp.dot(attended_low, proj_weight_all, preferred_element_type=jnp.float32)
        + proj_bias_all.astype(jnp.float32)
    )
    second_normed, mlp_back = jax.vjp(
        layer_norm,
        middle_residual,
        mlp_gain_all.astype(jnp.float32),
        mlp_shift_all.astype(jnp.float32),
    )
    second_low = second_normed.astype(jnp.bfloat16)
    inner_preactivation = jnp.dot(
        second_low, up_weight_all, preferred_element_type=jnp.float32
    ) + up_bias_all.astype(jnp.float32)
    active_hidden, gelu_back = jax.vjp(exact_gelu, inner_preactivation)
    active_low = active_hidden.astype(jnp.bfloat16)
    block_result = (
        middle_residual
        + jnp.dot(active_low, down_weight_all, preferred_element_type=jnp.float32)
        + down_bias_all.astype(jnp.float32)
    )
    block_out = block_result.astype(jnp.bfloat16).reshape(seqs_here, block_rows, feature_count)
    qkv_back, proj_back, up_back, down_back = (
        lax.all_gather(query_key_value_weight, "fsdp", axis=0, tiled=True),
        lax.all_gather(projection_output_weight, "fsdp", axis=0, tiled=True),
        lax.all_gather(up_projection_weight, "fsdp", axis=0, tiled=True),
        lax.all_gather(down_projection_weight, "fsdp", axis=0, tiled=True),
    )
    grad_top = out_grad.astype(jnp.float32).reshape(row_count, feature_count)
    branch_down = grad_top.astype(jnp.bfloat16)
    down_grad = jnp.einsum("rf,rd->fd", active_low, branch_down, preferred_element_type=jnp.float32)
    down_bias_grad = jnp.sum(branch_down, axis=0, dtype=jnp.float32)
    grad_active = jnp.einsum(
        "rd,fd->rf", branch_down, down_back, preferred_element_type=jnp.float32
    )
    inner_grad = gelu_back(grad_active)[0].astype(jnp.bfloat16)
    up_grad = jnp.einsum("rd,rf->df", second_low, inner_grad, preferred_element_type=jnp.float32)
    up_bias_grad = jnp.sum(inner_grad, axis=0, dtype=jnp.float32)
    grad_second = jnp.einsum("rf,df->rd", inner_grad, up_back, preferred_element_type=jnp.float32)
    grad_middle, mlp_gain_grad, mlp_shift_grad = mlp_back(grad_second)
    grad_middle = grad_middle + grad_top
    branch_up = grad_middle.astype(jnp.bfloat16)
    proj_grad = jnp.einsum("rd,re->de", attended_low, branch_up, preferred_element_type=jnp.float32)
    proj_bias_grad = jnp.sum(branch_up, axis=0, dtype=jnp.float32)
    att_grad = jnp.einsum(
        "re,de->rd", branch_up, proj_back, preferred_element_type=jnp.float32
    ).astype(jnp.bfloat16)
    grad_heads = att_grad.reshape(seqs_here, block_rows, HEADS, HD)
    row_delta = jnp.sum(
        attended_rows * jnp.transpose(grad_heads, (0, 2, 1, 3)).astype(jnp.float32), axis=-1
    )
    query_zero = jnp.zeros((seqs_here, HEADS, block_rows, HD), jnp.float32)
    back_state = (query_zero,)
    backward_step = partial(
        query_block,
        queries=query_heads,
        grad_out=grad_heads,
        row_stats=row_stats,
        row_delta=row_delta,
        query_pos=query_pos,
    )
    back_result = sweep_blocks(back_state, (keys_all, values_all), 0, block_rows, backward_step)
    query_grad = back_result[0]
    stats_all, delta_all = (
        lax.all_gather(
            jnp.transpose(row_stats, (0, 2, 1)).astype(jnp.bfloat16), "ctx", axis=1, tiled=True
        ).astype(jnp.float32),
        lax.all_gather(
            jnp.transpose(row_delta, (0, 2, 1)).astype(jnp.bfloat16), "ctx", axis=1, tiled=True
        ).astype(jnp.float32),
    )
    own_keys = split_heads(keys_seq)
    own_values = split_heads(values_seq)

    def key_step(carry_state, blocks, query_start):
        stats_blk = lax.dynamic_slice_in_dim(stats_all, query_start, block_rows, 1)
        delta_blk = lax.dynamic_slice_in_dim(delta_all, query_start, block_rows, 1)
        return key_block(
            carry_state,
            blocks[0],
            blocks[1],
            stats_blk,
            delta_blk,
            query_start,
            own_keys,
            own_values,
            query_pos,
        )

    key_zero = jnp.zeros((seqs_here, block_rows, HEADS, HD), jnp.float32)
    key_grad_own, value_grad_own = sweep_blocks(
        (key_zero, key_zero),
        (
            lax.all_gather(query_heads, "ctx", axis=1, tiled=True),
            lax.all_gather(grad_heads, "ctx", axis=1, tiled=True),
        ),
        jnp.int32(0),
        block_rows,
        key_step,
    )
    key_grad_sum = key_grad_own.reshape(seqs_here, block_rows, feature_count)
    value_grad_sum = value_grad_own.reshape(seqs_here, block_rows, feature_count)
    query_grad_low = (
        jnp.transpose(query_grad, (0, 2, 1, 3))
        .reshape(row_count, feature_count)
        .astype(jnp.bfloat16)
    )
    key_grad_low = key_grad_sum.reshape(row_count, feature_count).astype(jnp.bfloat16)
    value_grad_low = value_grad_sum.reshape(row_count, feature_count).astype(jnp.bfloat16)
    joined_grad = jnp.concatenate(
        [
            (query_grad_low.astype(jnp.float32) * 0.125).astype(jnp.bfloat16),
            key_grad_low,
            value_grad_low,
        ],
        axis=1,
    )
    qkv_grad = jnp.einsum("rd,rf->df", normed_low, joined_grad, preferred_element_type=jnp.float32)
    query_bias_grad = jnp.sum(query_grad_low, axis=0, dtype=jnp.float32) * 0.125
    value_bias_grad = jnp.sum(value_grad_low, axis=0, dtype=jnp.float32)
    grad_normed = jnp.einsum("rf,df->rd", joined_grad, qkv_back, preferred_element_type=jnp.float32)
    grad_hidden, attn_gain_grad, attn_shift_grad = attn_back(grad_normed)
    input_grad = (
        (grad_middle + grad_hidden)
        .astype(jnp.bfloat16)
        .reshape(seqs_here, block_rows, feature_count)
    )
    summed = (
        lax.psum_scatter(
            attn_gain_grad.astype(jnp.bfloat16), "fsdp", scatter_dimension=0, tiled=True
        ).astype(jnp.float32),
        lax.psum_scatter(
            attn_shift_grad.astype(jnp.bfloat16), "fsdp", scatter_dimension=0, tiled=True
        ).astype(jnp.float32),
        lax.psum_scatter(
            qkv_grad.astype(jnp.bfloat16), "fsdp", scatter_dimension=0, tiled=True
        ).astype(jnp.float32),
        lax.psum_scatter(
            query_bias_grad.astype(jnp.bfloat16), "fsdp", scatter_dimension=0, tiled=True
        ).astype(jnp.float32),
        lax.psum_scatter(
            value_bias_grad.astype(jnp.bfloat16), "fsdp", scatter_dimension=0, tiled=True
        ).astype(jnp.float32),
        lax.psum_scatter(
            proj_grad.astype(jnp.bfloat16), "fsdp", scatter_dimension=0, tiled=True
        ).astype(jnp.float32),
        lax.psum_scatter(
            proj_bias_grad.astype(jnp.bfloat16), "fsdp", scatter_dimension=0, tiled=True
        ).astype(jnp.float32),
        lax.psum_scatter(
            mlp_gain_grad.astype(jnp.bfloat16), "fsdp", scatter_dimension=0, tiled=True
        ).astype(jnp.float32),
        lax.psum_scatter(
            mlp_shift_grad.astype(jnp.bfloat16), "fsdp", scatter_dimension=0, tiled=True
        ).astype(jnp.float32),
        lax.psum_scatter(
            up_grad.astype(jnp.bfloat16), "fsdp", scatter_dimension=0, tiled=True
        ).astype(jnp.float32),
        lax.psum_scatter(
            up_bias_grad.astype(jnp.bfloat16), "fsdp", scatter_dimension=0, tiled=True
        ).astype(jnp.float32),
        lax.psum_scatter(
            down_grad.astype(jnp.bfloat16), "fsdp", scatter_dimension=0, tiled=True
        ).astype(jnp.float32),
        lax.psum_scatter(
            down_bias_grad.astype(jnp.bfloat16), "fsdp", scatter_dimension=0, tiled=True
        ).astype(jnp.float32),
    )
    summed = jax.tree.map(
        lambda part: part.astype(jnp.float32), lax.psum(as_sent(tuple(summed)), "ctx")
    )
    return (block_out, input_grad) + tuple(summed) + (row_stats,)


ROWS = 256


def low(value):
    return value.astype(jnp.bfloat16)


def wide(value):
    return value.astype(jnp.float32)


def dot(a, b):
    return jnp.dot(a, b, preferred_element_type=jnp.float32)


def xor_send(value, axis, bit, count):
    return lax.ppermute(value, axis, [(i, i ^ bit) for i in range(count)])


def shift_send(value, steps, count):
    return lax.ppermute(value, "ctx", [(i, (i + steps) % count) for i in range(count)])


def gather_fsdp(piece):
    me = lax.axis_index("fsdp")
    rows = piece.shape[0]
    half = rows // 2
    by_x = xor_send(piece, "fsdp", 2, 8)
    by_y = xor_send(piece, "fsdp", 4, 8)
    corner_top = xor_send(by_x[:half], "fsdp", 4, 8)
    corner_low = xor_send(by_y[half:], "fsdp", 2, 8)
    parts = [(0, 0, piece), (2, 0, by_x), (4, 0, by_y), (6, 0, corner_top), (6, half, corner_low)]
    whole = jnp.zeros((8 * rows,) + piece.shape[1:], piece.dtype)
    for place, offset, part in parts:
        other = xor_send(part, "fsdp", 1, 8)
        start = jnp.bitwise_xor(me, place) * rows + offset
        whole = lax.dynamic_update_slice_in_dim(whole, part, start, 0)
        start = jnp.bitwise_xor(me, place + 1) * rows + offset
        whole = lax.dynamic_update_slice_in_dim(whole, other, start, 0)
    return whole


def scatter_fsdp(grad):
    me = lax.axis_index("fsdp")
    core, x, y = me % 2, (me // 2) % 2, me // 4
    rows, columns = grad.shape
    blocks = grad.reshape(2, 2, 2, rows // 8, columns)
    kept = lax.dynamic_index_in_dim(blocks, core, 2, keepdims=False)
    sent = low(lax.dynamic_index_in_dim(blocks, 1 - core, 2, keepdims=False))
    total = low(wide(kept) + wide(xor_send(sent, "fsdp", 1, 8)))
    half = rows // 16
    top, bottom = total[:, :, :half], total[:, :, half:]

    def fold(part, axis, place, bit):
        keep = lax.dynamic_index_in_dim(part, place, axis, keepdims=False)
        send = lax.dynamic_index_in_dim(part, 1 - place, axis, keepdims=False)
        return low(wide(keep) + wide(xor_send(send, "fsdp", bit, 8)))

    top = fold(fold(top, 1, x, 2), 0, y, 4)
    bottom = fold(fold(bottom, 0, y, 4), 0, x, 2)
    return jnp.concatenate([top, bottom], axis=0)


def sum_ctx(part):
    me = lax.axis_index("ctx")
    odd = me % 2
    rows = part.shape[0]
    halves = part.reshape((2, rows // 2) + part.shape[1:])
    keep = lax.dynamic_index_in_dim(halves, odd, 0, keepdims=False)
    send = lax.dynamic_index_in_dim(halves, 1 - odd, 0, keepdims=False)
    own = low(wide(keep) + wide(xor_send(send, "ctx", 1, 4)))
    own = low(wide(own) + wide(xor_send(own, "ctx", 2, 4)))
    other = xor_send(own, "ctx", 1, 4)
    return jnp.where(odd == 0, jnp.concatenate([own, other]), jnp.concatenate([other, own]))


def gather_ctx(block):
    me = lax.axis_index("ctx")
    whole = jnp.zeros((4,) + block.shape, block.dtype)
    whole = lax.dynamic_update_index_in_dim(whole, block, me, 0)
    right = left = block
    for step in range(1, 4):
        right = lax.ppermute(right, "ctx", [(i, i + 1) for i in range(step - 1, 3)])
        left = lax.ppermute(left, "ctx", [(i, i - 1) for i in range(1, 5 - step)])
        source = (me - step) % 4
        other = (me + step) % 4
        whole = lax.dynamic_update_index_in_dim(
            whole,
            jnp.where(me >= step, right, lax.dynamic_index_in_dim(whole, source, 0, keepdims=False)),
            source,
            0,
        )
        whole = lax.dynamic_update_index_in_dim(
            whole,
            jnp.where(me + step < 4, left, lax.dynamic_index_in_dim(whole, other, 0, keepdims=False)),
            other,
            0,
        )
    return whole.reshape((-1,) + block.shape[1:])


def scatter_ctx(total):
    me = lax.axis_index("ctx")

    def block(index):
        return lax.dynamic_index_in_dim(total, jnp.clip(index, 0, 3), 0, keepdims=False)

    right = left = None
    for step in range(3):
        going_right, going_left = block(3 - step + me), block(step - 3 + me)
        if step:
            going_right = wide(going_right) + wide(right)
            going_left = wide(going_left) + wide(left)
        right = lax.ppermute(low(going_right), "ctx", [(i, i + 1) for i in range(step + 1)])
        left = lax.ppermute(low(going_left), "ctx", [(i, i - 1) for i in range(3 - step, 4)])
    return wide(block(me)) + wide(right) + wide(left)


def heads_to_positions(value, ordered_axis):
    me = lax.axis_index("ctx")
    result = jnp.zeros(value.shape, value.dtype)
    result = lax.dynamic_update_index_in_dim(
        result, lax.dynamic_index_in_dim(value, me, 0, keepdims=False), me, 0
    )
    for step in (2, 1, 3):
        piece = lax.dynamic_index_in_dim(value, (me + step) % 4, 0, keepdims=False)
        result = lax.dynamic_update_index_in_dim(
            result, shift_send(piece, step, 4), (me - step) % 4, 0
        )
    return jnp.moveaxis(result, 0, ordered_axis)


def masked_scores(keys, queries_t, tile):
    scores = dot(keys, queries_t)
    key_pos = lax.broadcasted_iota(jnp.int32, (ROWS, ROWS), 0)
    query_pos = lax.broadcasted_iota(jnp.int32, (ROWS, ROWS), 1)
    diagonal = jnp.where(key_pos <= query_pos, scores[tile * ROWS :], NEG_BIG)
    if tile == 0:
        return diagonal
    return jnp.concatenate([scores[: tile * ROWS], diagonal], axis=0)


def attend_kernel(qkv_ref, out_ref, stats_ref):
    length, width = out_ref.shape
    heads = width // HD
    queries_t = qkv_ref[:, :width].T
    values_t = qkv_ref[:, 2 * width :].T
    for head in range(heads):
        keys = qkv_ref[:, width + head * HD : width + (head + 1) * HD]
        lanes = slice(head * HD, (head + 1) * HD)
        for tile in range(length // ROWS):
            rows = slice(tile * ROWS, (tile + 1) * ROWS)
            seen = (tile + 1) * ROWS
            scores = masked_scores(keys[:seen], queries_t[lanes, rows], tile)
            top = jnp.max(scores, axis=0, keepdims=True)
            weights = jnp.exp(scores - top)
            total = jnp.sum(weights, axis=0, keepdims=True)
            mixed = dot(values_t[lanes, :seen], low(weights)) / total
            out_ref[rows, lanes] = mixed.T
            stats_ref[head : head + 1, rows] = top + jnp.log(total)


def attend_back_kernel(qkv_ref, att_ref, grad_ref, stats_ref, out_ref, key_ref, value_ref):
    length, width = att_ref.shape
    heads = width // HD
    queries_t = qkv_ref[:, :width].T
    keys_t = qkv_ref[:, width : 2 * width].T
    grad_t = grad_ref[...].T
    product_t = (att_ref[...] * wide(grad_ref[...])).T
    for head in range(heads):
        lanes = slice(head * HD, (head + 1) * HD)
        queries = qkv_ref[:, head * HD : (head + 1) * HD]
        keys = qkv_ref[:, width + head * HD : width + (head + 1) * HD]
        values = qkv_ref[:, 2 * width + head * HD : 2 * width + (head + 1) * HD]
        grads = grad_ref[:, lanes]
        delta = jnp.sum(product_t[lanes], axis=0, keepdims=True)
        key_ref[...] = jnp.zeros_like(key_ref)
        value_ref[...] = jnp.zeros_like(value_ref)
        for tile in range(length // ROWS):
            rows = slice(tile * ROWS, (tile + 1) * ROWS)
            seen = (tile + 1) * ROWS
            scores = masked_scores(keys[:seen], queries_t[lanes, rows], tile)
            prob = jnp.exp(scores - stats_ref[head : head + 1, rows])
            prob_grad = dot(values[:seen], grad_t[lanes, rows])
            score_grad = low(prob * (prob_grad - delta[:, rows]))
            query_grad = dot(keys_t[lanes, :seen], score_grad)
            out_ref[rows, lanes] = low(low(query_grad).T * jnp.bfloat16(0.125))
            key_ref[:seen] += dot(score_grad, queries[rows])
            value_ref[:seen] += dot(low(prob), grads[rows])
        out_ref[:, width + head * HD : width + (head + 1) * HD] = low(key_ref[...])
        out_ref[:, 2 * width + head * HD : 2 * width + (head + 1) * HD] = low(value_ref[...])


def attend(qkv):
    length, width = qkv.shape[0], qkv.shape[1] // 3
    return pl.pallas_call(
        attend_kernel,
        out_shape=(
            jax.ShapeDtypeStruct((length, width), jnp.float32),
            jax.ShapeDtypeStruct((width // HD, length), jnp.float32),
        ),
        compiler_params=pltpu.CompilerParams(vmem_limit_bytes=40 * 1024 * 1024),
        cost_estimate=pl.CostEstimate(
            flops=8 * length * length * width, bytes_accessed=4 * length * width * 4, transcendentals=2 * length * length
        ),
    )(qkv)


def attend_back(qkv, attended, grads, stats):
    length, width = attended.shape
    return pl.pallas_call(
        attend_back_kernel,
        out_shape=jax.ShapeDtypeStruct((length, 3 * width), jnp.bfloat16),
        scratch_shapes=[pltpu.VMEM((length, HD), jnp.float32), pltpu.VMEM((length, HD), jnp.float32)],
        compiler_params=pltpu.CompilerParams(vmem_limit_bytes=40 * 1024 * 1024),
        cost_estimate=pl.CostEstimate(
            flops=20 * length * length * width, bytes_accessed=5 * length * width * 4, transcendentals=2 * length * length
        ),
    )(qkv, attended, grads, stats)


def norm_parts(values):
    center = values - jnp.mean(values, axis=-1, keepdims=True)
    inverse = lax.rsqrt(jnp.mean(center * center, axis=-1, keepdims=True) + 1e-05)
    return center * inverse, inverse


def norm_back(grad, unit, inverse, gain):
    inner = grad * gain
    mean_inner = jnp.mean(inner, axis=-1, keepdims=True)
    mean_product = jnp.mean(inner * unit, axis=-1, keepdims=True)
    return (
        inverse * (inner - mean_inner - unit * mean_product),
        jnp.sum(grad * unit, axis=0),
        jnp.sum(grad, axis=0),
    )


def local_fast(
    hidden_in,
    attn_gain,
    attn_shift,
    query_key_value_weight,
    query_bias,
    value_bias,
    projection_output_weight,
    projection_output_bias,
    mlp_gain,
    mlp_shift,
    up_projection_weight,
    up_projection_bias,
    down_projection_weight,
    down_projection_bias,
    out_grad,
):
    seqs, block_rows, width = hidden_in.shape
    place = lax.axis_index("ctx")
    share = width // 4
    row_count = seqs * block_rows
    shard = width // 8

    vectors = jnp.stack(
        [attn_gain, attn_shift, query_bias, value_bias, projection_output_bias, mlp_gain, mlp_shift, down_projection_bias]
        + list(up_projection_bias.reshape(4, shard))
        + [attn_gain] * 4
    )
    flat = jnp.pad(vectors.reshape(-1), (0, 16 * 3 * share - 16 * shard)).reshape(16, 3 * share)

    def heads_here(array):
        return lax.dynamic_slice_in_dim(array, place * share, share, array.ndim - 1)

    qkv_own = heads_here(query_key_value_weight.reshape(shard, 3, width)).reshape(shard, 3 * share)
    first = gather_fsdp(jnp.concatenate([qkv_own, flat])).reshape(8, shard + 16, 3 * share)
    qkv_all = first[:, :shard].reshape(width, 3 * share)
    vectors_all = wide(first[:, shard:].reshape(8, -1)[:, : 16 * shard].reshape(8, 16, shard))
    (gain_1, shift_1, bias_q, bias_v, bias_proj, gain_2, shift_2, bias_down) = (
        vectors_all[:, i].reshape(width) for i in range(8)
    )
    bias_up = vectors_all[:, 8:12].reshape(4 * width)

    hidden_all = gather_ctx(hidden_in).reshape(4, seqs, block_rows, width)
    full = [hidden_all[:, s].reshape(4 * block_rows, width) for s in range(seqs)]
    up_parts = [up_projection_weight[:, k * width : (k + 1) * width] for k in range(4)]
    later = gather_fsdp(jnp.concatenate(up_parts + [down_projection_weight, projection_output_weight]))
    later = later.reshape(8, 9 * shard, width)
    up_all = jnp.concatenate(
        [later[:, k * shard : (k + 1) * shard].reshape(width, width) for k in range(4)], axis=1
    )
    down_all = later[:, 4 * shard : 8 * shard].reshape(4 * width, width)
    proj_all = later[:, 8 * shard :].reshape(width, width)

    bias_qkv = jnp.concatenate([heads_here(bias_q), jnp.zeros((share,), jnp.float32), heads_here(bias_v)])
    scale = jnp.concatenate([jnp.full((share,), 0.125, jnp.float32), jnp.ones((2 * share,), jnp.float32)])
    normed, qkv, attended, stats, blocks = [], [], [], [], []
    for s in range(seqs):
        unit, unused = norm_parts(wide(full[s]))
        normed.append(low(unit * gain_1 + shift_1))
        qkv.append(low((dot(normed[s], qkv_all) + bias_qkv) * scale))
        att, stat = attend(qkv[s])
        attended.append(att)
        stats.append(stat)
        blocks.append(low(att).reshape(4, block_rows, share))
    stats_all = jnp.stack(stats)
    heads_each = stats_all.shape[1]
    stats_out = heads_to_positions(
        jnp.moveaxis(stats_all.reshape(seqs, heads_each, 4, block_rows), 2, 0), 1
    ).reshape(seqs, 4 * heads_each, block_rows)
    attended_low = heads_to_positions(jnp.stack(blocks, axis=1), 2).reshape(row_count, width)

    hidden = wide(hidden_in).reshape(row_count, width)
    middle = hidden + dot(attended_low, proj_all) + bias_proj
    unit_2, inverse_2 = norm_parts(middle)
    second = low(unit_2 * gain_2 + shift_2)
    inner = dot(second, up_all) + bias_up
    below = 0.5 * (1.0 + lax.erf(inner * 0.7071067811865476))
    active = low(inner * below)
    slope = below + inner * (jnp.exp(-0.5 * inner * inner) * 0.3989422804014327)
    block_out = low(middle + dot(active, down_all) + bias_down).reshape(seqs, block_rows, width)

    branch_down = out_grad.reshape(row_count, width)
    top = wide(branch_down)
    contract_rows = (((0,), (0,)), ((), ()))
    contract_columns = (((1,), (1,)), ((), ()))

    def weight_grad(a, b):
        return lax.dot_general(a, b, contract_rows, preferred_element_type=jnp.float32)

    def through(a, b):
        return lax.dot_general(a, b, contract_columns, preferred_element_type=jnp.float32)

    down_grad = low(weight_grad(active, branch_down))
    inner_grad = low(through(branch_down, down_all) * slope)
    up_grad = low(weight_grad(second, inner_grad)).reshape(8, shard, 4 * width)
    grad_middle, gain_2_grad, shift_2_grad = norm_back(through(inner_grad, up_all), unit_2, inverse_2, gain_2)
    grad_middle = grad_middle + top
    branch_up = low(grad_middle)
    att_grad = low(through(branch_up, proj_all))
    proj_grad = low(weight_grad(attended_low, branch_up))
    grads_all = jnp.concatenate(
        [up_grad[:, :, k * width : (k + 1) * width] for k in range(4)]
        + [down_grad.reshape(8, 4 * shard, width), proj_grad.reshape(8, shard, width)],
        axis=1,
    )
    grads_sum = sum_ctx(scatter_fsdp(grads_all.reshape(8 * 9 * shard, width)))
    up_grad = jnp.concatenate([grads_sum[k * shard : (k + 1) * shard] for k in range(4)], axis=1)
    down_grad, proj_grad = grads_sum[4 * shard : 8 * shard], grads_sum[8 * shard :]

    att_grad = jnp.moveaxis(att_grad.reshape(seqs, block_rows, 4, share), 2, 0)
    att_grad = heads_to_positions(att_grad, 1)
    joined, partials = [], []
    qkv_grad = 0.0
    for s in range(seqs):
        grads = att_grad[s].reshape(4 * block_rows, share)
        joined.append(attend_back(qkv[s], attended[s], grads, stats[s]))
        partials.append(low(through(joined[s], qkv_all)).reshape(4, block_rows, width))
        qkv_grad = qkv_grad + weight_grad(normed[s], joined[s])
    own_grad = scatter_ctx(jnp.stack(partials, axis=1).reshape(4, row_count, width))

    joined_all = jnp.concatenate(joined)
    bias_sums = jnp.sum(joined_all, axis=0, dtype=jnp.float32)
    zero_row = jnp.zeros((width,), jnp.float32)
    query_bias_grad = lax.dynamic_update_slice_in_dim(zero_row, bias_sums[:share], place * share, 0)
    value_bias_grad = lax.dynamic_update_slice_in_dim(zero_row, bias_sums[2 * share :], place * share, 0)

    unit_1, inverse_1 = norm_parts(hidden)
    grad_hidden, gain_1_grad, shift_1_grad = norm_back(own_grad, unit_1, inverse_1, gain_1)
    input_grad = low(grad_middle + grad_hidden).reshape(seqs, block_rows, width)

    rows = [
        gain_1_grad,
        shift_1_grad,
        query_bias_grad,
        value_bias_grad,
        jnp.sum(branch_up, axis=0, dtype=jnp.float32),
        gain_2_grad,
        shift_2_grad,
        jnp.sum(branch_down, axis=0, dtype=jnp.float32),
    ]
    up_bias_grad = jnp.sum(inner_grad, axis=0, dtype=jnp.float32)
    small = jnp.concatenate(
        [
            jnp.stack(rows).reshape(8, 8, shard).transpose(1, 0, 2),
            up_bias_grad.reshape(8, 4, shard),
            jnp.zeros((8, 4, shard), jnp.float32),
        ],
        axis=1,
    )
    small = jnp.pad(low(small).reshape(8, 16 * shard), ((0, 0), (0, 16 * 3 * share - 16 * shard)))
    last = jnp.concatenate([low(qkv_grad).reshape(8, shard, 3 * share), small.reshape(8, 16, 3 * share)], axis=1)
    last = scatter_fsdp(last.reshape(8 * (shard + 16), 3 * share))
    pieces = jnp.zeros((4,) + last.shape, last.dtype)
    pieces = lax.dynamic_update_index_in_dim(pieces, last, place, 0)
    for step in (2, 1, 3):
        pieces = lax.dynamic_update_index_in_dim(pieces, shift_send(last, step, 4), (place - step) % 4, 0)
    qkv_out = wide(
        jnp.moveaxis(pieces[:, :shard].reshape(4, shard, 3, share), 0, 2).reshape(shard, 3 * width)
    )
    small = jnp.sum(wide(pieces[:, shard:]), axis=0).reshape(-1)[: 16 * shard].reshape(16, shard)
    return (
        block_out,
        input_grad,
        small[0],
        small[1],
        qkv_out,
        small[2],
        small[3],
        wide(proj_grad),
        small[4],
        small[5],
        small[6],
        wide(up_grad),
        small[8:12].reshape(4 * shard),
        wide(down_grad),
        small[7],
        stats_out,
    )


def solution(mesh):
    fast = mesh.shape["ctx"] == 4 and mesh.shape["fsdp"] == 8
    chosen = local_fast if fast else local_general
    placed = (
        P("fsdp", "ctx", None),
        P("fsdp"),
        P("fsdp"),
        P("fsdp", None),
        P("fsdp"),
        P("fsdp"),
        P("fsdp", None),
        P("fsdp"),
        P("fsdp"),
        P("fsdp"),
        P("fsdp", None),
        P("fsdp"),
        P("fsdp", None),
        P("fsdp"),
        P("fsdp", "ctx", None),
    )
    return jax.shard_map(
        chosen,
        mesh=mesh,
        in_specs=placed,
        out_specs=(
            P("fsdp", "ctx", None),
            P("fsdp", "ctx", None),
            P("fsdp"),
            P("fsdp"),
            P("fsdp", None),
            P("fsdp"),
            P("fsdp"),
            P("fsdp", None),
            P("fsdp"),
            P("fsdp"),
            P("fsdp"),
            P("fsdp", None),
            P("fsdp"),
            P("fsdp", None),
            P("fsdp"),
            P("fsdp", None, "ctx"),
        ),
        check_vma=False,
    )
```
